32 devices in a mesh: groups: 2 (over y), owner: 16 (over z, x, core).
Axes of the slice: x: 2, y: 2, z: 4, core: 2. Of those that a mesh axis runs over, the one named last changes fastest.
Arguments:
- token_input_rows: bfloat16 [4096, 4096], P(('groups', 'owner')), parts along dimension 0, may hold values from -6 to 6
- output_gradient_rows: bfloat16 [4096, 1024], P(('groups', 'owner')), parts along dimension 0, may hold values from -6 to 6
- token_tenant_index: int32 [4096], P(('groups', 'owner')), parts along dimension 0, may hold values from 0 to 31, as said below
- tenant_slot_index: int32 [64], P('groups'), parts along dimension 0, may hold values from 0 to 31, as said below
- key_matrix: bfloat16 [4096, 1024], P('owner'), may hold values from -0.09375 to 0.09375
- adapter_down_weight: bfloat16 [4096, 4096], P(None, ('groups', 'owner')), parts along dimension 1, may hold values from -0.09375 to 0.09375
- adapter_up_weight: bfloat16 [4096, 1024], P(('groups', 'owner')), parts along dimension 0, may hold values from -0.75 to 0.75
Outputs:
- input_grads: bfloat16 [4096, 4096], P(('groups', 'owner')), parts along dimension 0
- down_grads: bfloat16 [4096, 4096], P(None, ('groups', 'owner')), parts along dimension 1
- up_grads: bfloat16 [4096, 1024], P(('groups', 'owner')), parts along dimension 0
The draws below stay inside these ranges and needn't reach their ends.
There are 2 independent parts, one for each index of `groups`. The reference program is written for one: setup_inputs(seed, part) draws one part's arguments, and reference() takes and returns one part's arrays. A program takes and returns all parts, laid end to end along the dimension named above; an argument that names none is the same for every part. Nothing has to cross between parts.
Inputs may be any that keep to these rules, and one draw needn't show every extreme that they name: `token_tenant_index`: the tokens of one device (aligned blocks of 128) name tenants of at most 16 tokens a holding device, where tenant k is held by device tenant_slot_index[k] // 2; in every draw one holding device gets exactly 16 tokens from every device. `tenant_slot_index`: A permutation of the slots.
All inputs are finite; a program needn't handle non-finite values.
Results may differ from the reference program's by a relative error of at most 0.0055.
Values may be sent and summed in bfloat16 or wider, within the bound.
A program may use at most 64 MiB of HBM per device.

```python
import jax
import jax.numpy as jnp
from jax import lax

MODEL_WIDTH = 4096
KEY_WIDTH = 1024
ADAPTER_RANK = 64
TOK_DEV = 128
TEN_DEV = 2
TENANT_COUNT = 32
TOKENS = 2048
CAP = 16
N_OWNER = 16


def shared_slots(key):
    return jax.random.permutation(jax.random.fold_in(key, 11), TENANT_COUNT).astype(jnp.int32)


def draw_tenant_slot_index(key, part):
    return shared_slots(key)


def draw_token_tenant_index(key, part):
    slots = shared_slots(key)
    tenant_at = jnp.argsort(slots, stable=True).astype(jnp.int32)
    key = jax.random.fold_in(key, 5)
    keys = jax.random.split(key, 5)
    total_slots = N_OWNER * CAP
    busiest = jax.random.randint(keys[0], (), 0, N_OWNER)
    level = jax.random.randint(keys[1], (N_OWNER, N_OWNER), 0, 4)
    level = jnp.where(jnp.arange(N_OWNER)[None, :] == busiest, 400, level)
    slot_owner = jnp.arange(total_slots, dtype=jnp.int32) // CAP
    noise = jax.random.randint(keys[2], (N_OWNER, total_slots), 0, 1024)
    score = (level[:, slot_owner] * 1024 + noise) * total_slots + jnp.arange(total_slots, dtype=jnp.int32)[None, :]
    chosen = lax.top_k(score, TOK_DEV)[1].astype(jnp.int32)
    holders = chosen // CAP
    mixing = jax.random.randint(keys[3], (N_OWNER, TOK_DEV), 0, 1 << 20) * TOK_DEV + jnp.arange(TOK_DEV, dtype=jnp.int32)[None, :]
    shuffle = jnp.argsort(mixing, axis=1).astype(jnp.int32)
    holders = jnp.take_along_axis(holders, shuffle, axis=1)
    within = jax.random.randint(keys[4], (N_OWNER, TOK_DEV), 0, TEN_DEV)
    return tenant_at[holders * TEN_DEV + within].reshape(-1).astype(jnp.int32)


def steps_of(rng, extent, shards, least, high):
    gain, own = 1.0, jax.random.fold_in(rng, 6)
    for axis_at, parts in shards:
        heights = jnp.exp(jax.random.uniform(jax.random.fold_in(own, axis_at), (parts,), jnp.float32, least / len(shards), high / len(shards)))
        gain = gain * jnp.repeat(heights, extent[axis_at] // parts).reshape([-1 if axis == axis_at else 1 for axis in range(len(extent))])
    return gain


def normal_values(own_key, shape, spread, reach, cuts=(), kind=jnp.bfloat16):
    gain = steps_of(own_key, shape, cuts, -0.22, 0.18) if cuts else 1.0
    entries = jax.random.normal(own_key, shape, jnp.float32) * spread * gain
    return jnp.minimum(jnp.maximum(entries, -reach), reach).astype(kind)


def setup_inputs(seed: int = 0, part: int = 0) -> dict:
    key_of = jax.random.split(jax.random.key(seed), 8)
    part_keys = jax.random.split(jax.random.fold_in(key_of[7], part), 8)
    return {
        "token_input_rows": normal_values(part_keys[0], (TOKENS, MODEL_WIDTH), 1.0, 6.0, ((0, 16),)),
        "output_gradient_rows": normal_values(part_keys[1], (TOKENS, KEY_WIDTH), 1.0, 6.0, ((0, 16),)),
        "token_tenant_index": draw_token_tenant_index(jax.random.fold_in(jax.random.fold_in(key_of[7], part), 71), part),
        "tenant_slot_index": draw_tenant_slot_index(jax.random.fold_in(jax.random.fold_in(key_of[7], part), 71), part),
        "key_matrix": normal_values(key_of[4], (MODEL_WIDTH, KEY_WIDTH), MODEL_WIDTH ** -0.5, 0.09375, ((0, 16),)),
        "adapter_down_weight": normal_values(part_keys[5], (MODEL_WIDTH, TENANT_COUNT * ADAPTER_RANK), MODEL_WIDTH ** -0.5, 0.09375, ((1, 16),)),
        "adapter_up_weight": normal_values(part_keys[6], (TENANT_COUNT * ADAPTER_RANK, KEY_WIDTH), ADAPTER_RANK ** -0.5, 0.75, ((0, 16),)),
    }


adapter_scale = 2.0
gradient_norm = 1.0 / 64.0


def reference(token_input_rows, output_gradient_rows, token_tenant_index, tenant_slot_index, key_matrix, adapter_down_weight, adapter_up_weight):
    buffer_rows = N_OWNER * CAP
    slot_of = tenant_slot_index[token_tenant_index].astype(jnp.int32)
    order = jnp.argsort(slot_of, stable=True).astype(jnp.int32)
    counts = jnp.sum((slot_of[:, None] == jnp.arange(TENANT_COUNT, dtype=jnp.int32)[None, :]).astype(jnp.int32), axis=0)
    starts = (jnp.cumsum(counts) - counts).astype(jnp.int32)
    width = token_input_rows.shape[1]
    sorted_x = jnp.concatenate([token_input_rows[order], jnp.zeros((buffer_rows, width), token_input_rows.dtype)], 0)
    sorted_g = jnp.concatenate([output_gradient_rows[order], jnp.zeros((buffer_rows, KEY_WIDTH), output_gradient_rows.dtype)], 0)

    def one_slot(carry, adapter_slot):
        begin = starts[adapter_slot]
        x_block = lax.dynamic_slice_in_dim(sorted_x, begin, buffer_rows, 0)
        gradient_block = lax.dynamic_slice_in_dim(sorted_g, begin, buffer_rows, 0)
        valid_mask = (jnp.arange(buffer_rows, dtype=jnp.int32) < counts[adapter_slot])[:, None]
        down_matrix = lax.dynamic_slice_in_dim(adapter_down_weight, adapter_slot * ADAPTER_RANK, ADAPTER_RANK, 1)
        up_matrix = lax.dynamic_slice_in_dim(adapter_up_weight, adapter_slot * ADAPTER_RANK, ADAPTER_RANK, 0)
        reduced_input = jnp.where(valid_mask, jnp.dot(x_block, down_matrix, preferred_element_type=jnp.float32), 0.0).astype(jnp.bfloat16)
        backward_pass = lax.dot_general(gradient_block, up_matrix, (((1,), (1,)), ((), ())), preferred_element_type=jnp.float32)
        reduced_gradient = jnp.where(valid_mask, adapter_scale * backward_pass, 0.0).astype(jnp.bfloat16)
        down_grad = (gradient_norm * lax.dot_general(x_block, reduced_gradient, (((0,), (0,)), ((), ())), preferred_element_type=jnp.float32)).astype(jnp.bfloat16)
        up_gradient = (adapter_scale * gradient_norm * lax.dot_general(reduced_input, gradient_block, (((0,), (0,)), ((), ())), preferred_element_type=jnp.float32)).astype(jnp.bfloat16)
        part = lax.dot_general(reduced_gradient, down_matrix, (((1,), (1,)), ((), ())), preferred_element_type=jnp.float32).astype(jnp.bfloat16)
        current = lax.dynamic_slice_in_dim(carry, begin, buffer_rows, 0)
        carry = lax.dynamic_update_slice_in_dim(carry, jnp.where(valid_mask, part, current), begin, 0)
        return carry, (down_grad, up_gradient)

    initial = jnp.zeros((TOKENS + buffer_rows, width), jnp.bfloat16)
    parts_sorted, (down_all, up_all) = lax.scan(one_slot, initial, jnp.arange(TENANT_COUNT, dtype=jnp.int32))
    adapter_part = jnp.zeros((TOKENS, width), jnp.bfloat16).at[order].set(parts_sorted[:TOKENS])
    base = lax.dot_general(output_gradient_rows, key_matrix, (((1,), (1,)), ((), ())), preferred_element_type=jnp.float32)
    input_grads = (base + adapter_part.astype(jnp.float32)).astype(jnp.bfloat16)
    down_grads = jnp.transpose(down_all, (1, 0, 2)).reshape(width, TENANT_COUNT * ADAPTER_RANK)
    up_grads = up_all.reshape(TENANT_COUNT * ADAPTER_RANK, KEY_WIDTH)
    return (input_grads, down_grads, up_grads)
```

```python
import functools

import jax
import jax.numpy as jnp
from jax import lax
from jax.experimental import pallas as pl
from jax.experimental.pallas import tpu as pltpu
from jax.sharding import PartitionSpec as P

ADAPTER_RANK = 64
TEN_DEV = 2


adapter_scale = 2.0
gradient_norm = 1.0 / 64.0


def slot_holder_products(
    received_input, received_gradient, received_tenant, adapter_down_weight, adapter_up_weight
):
    column_tenant = jnp.arange(TEN_DEV * ADAPTER_RANK, dtype=jnp.int32) // ADAPTER_RANK
    valid_mask = received_tenant[:, None] == column_tenant[None, :]
    reduced_input = jnp.where(
        valid_mask,
        jnp.dot(received_input, adapter_down_weight, preferred_element_type=jnp.float32),
        0.0,
    ).astype(jnp.bfloat16)
    backward_pass = lax.dot_general(
        received_gradient,
        adapter_up_weight,
        (((1,), (1,)), ((), ())),
        preferred_element_type=jnp.float32,
    )
    reduced_gradient = jnp.where(valid_mask, adapter_scale * backward_pass, 0.0).astype(
        jnp.bfloat16
    )
    down_grads = (
        gradient_norm
        * lax.dot_general(
            received_input,
            reduced_gradient,
            (((0,), (0,)), ((), ())),
            preferred_element_type=jnp.float32,
        )
    ).astype(jnp.bfloat16)
    up_grads = (
        adapter_scale
        * gradient_norm
        * lax.dot_general(
            reduced_input,
            received_gradient,
            (((0,), (0,)), ((), ())),
            preferred_element_type=jnp.float32,
        )
    ).astype(jnp.bfloat16)
    adapter_part = lax.dot_general(
        reduced_gradient,
        adapter_down_weight,
        (((1,), (1,)), ((), ())),
        preferred_element_type=jnp.float32,
    ).astype(jnp.bfloat16)
    return (adapter_part, down_grads, up_grads)


def frozen_product(output_gradient_rows, key_matrix):
    return lax.dot_general(
        output_gradient_rows,
        lax.all_gather(key_matrix, "owner", axis=0, tiled=True),
        (((1,), (1,)), ((), ())),
        preferred_element_type=jnp.float32,
    )


MESH = pl.DeviceIdType.MESH
NT = (((1,), (1,)), ((), ()))
TN = (((0,), (0,)), ((), ()))
COLUMNS = 512
RING = 8


def matmul(a, b, dims=(((1,), (0,)), ((), ()))):
    return lax.dot_general(a, b, dims, preferred_element_type=jnp.float32)


def ring_chip(position):
    up = (position < 4).astype(jnp.int32)
    z = up * position + (1 - up) * (7 - position)
    return z * 2 + (1 - up)


def fused_kernel(
    n,
    cap,
    place_ref,
    place_t_ref,
    local_ref,
    x_ref,
    g_ref,
    k_ref,
    down_ref,
    up_ref,
    out_ref,
    down_grads_ref,
    up_grads_ref,
    x_send,
    x_recv,
    g_send,
    g_recv,
    part,
    returned,
    key,
    base,
    reduced,
    h_sum,
    gs_sem,
    gr_sem,
    xs_sem,
    xr_sem,
    ps_sem,
    pr_sem,
    ks_sem,
    kr_sem,
):
    group = lax.axis_index("groups")
    me = lax.axis_index("owner")
    width = x_ref.shape[1]
    grad = g_ref.shape[1]
    tiles = width // COLUMNS
    core = me % 2
    chip = me // 2
    z, x = chip // 2, chip % 2
    position = (1 - x) * z + x * (7 - z)
    step_by = 1 - 2 * core
    sibling = (group, chip * 2 + 1 - core)
    across = (1 - group, me)
    ahead = (group, ring_chip((position + step_by + RING) % RING) * 2 + core)

    barrier = pltpu.get_barrier_semaphore()

    @pl.loop(1, n)
    def _(i):
        pl.semaphore_signal(barrier, inc=1, device_id=(group, (me + i) % n), device_id_type=MESH)

    pl.semaphore_signal(barrier, inc=1, device_id=across, device_id_type=MESH)

    def rows_of(owner):
        return pl.ds(pl.multiple_of(owner * cap, cap), cap)

    def row_copy(src, dst, send, recv, at, owner, i):
        return pltpu.make_async_remote_copy(
            src_ref=src.at[rows_of(owner)],
            dst_ref=dst.at[rows_of(at)],
            send_sem=send.at[i],
            recv_sem=recv.at[i],
            device_id=(group, owner),
            device_id_type=MESH,
        )

    def start_all(src, dst, send, recv):
        @pl.loop(1, n)
        def _(i):
            row_copy(src, dst, send, recv, me, (me + i) % n, i).start()

    def wait_arrivals(src, dst, send, recv):
        @pl.loop(1, n)
        def _(i):
            row_copy(src, dst, send, recv, (me + n - i) % n, (me + i) % n, i).wait_recv()

    def wait_sent(src, dst, send, recv):
        @pl.loop(1, n)
        def _(i):
            row_copy(src, dst, send, recv, me, (me + i) % n, i).wait_send()

    half = k_ref.shape[0] // 2

    def key_rows(at_position, of_core, of_half):
        owner = ring_chip(at_position) * 2 + of_core
        return pl.ds(pl.multiple_of((owner * 2 + of_half) * half, half), half)

    def key_copy(rows, sem, device, src=None):
        return pltpu.make_async_remote_copy(
            src_ref=key.at[rows] if src is None else src,
            dst_ref=key.at[rows],
            send_sem=ks_sem.at[sem],
            recv_sem=kr_sem.at[sem],
            device_id=device,
            device_id_type=MESH,
        )

    def origin(s):
        return (position + (RING - s) * step_by + 2 * RING * RING) % RING

    def sibling_origin(s):
        return (position - (RING - s) * step_by + 2 * RING * RING) % RING

    def ring_copy(s):
        if s == 0:
            return key_copy(
                key_rows(position, core, group),
                0,
                ahead,
                k_ref.at[pl.ds(pl.multiple_of(group * half, half), half)],
            )
        return key_copy(key_rows(origin(s), core, group), s, ahead)

    def ring_arrival(s):
        return key_copy(key_rows(origin(s + 1), core, group), s, ahead)

    def across_copy(s):
        return key_copy(key_rows(origin(s + 1), core, group), 7 + s, across)

    def across_arrival(s):
        return key_copy(key_rows(origin(s + 1), core, 1 - group), 7 + s, across)

    def sibling_copy(s, far):
        return key_copy(
            key_rows(origin(s + 1), core, 1 - group if far else group), (21 if far else 14) + s, sibling
        )

    def sibling_arrival(s, far):
        return key_copy(
            key_rows(sibling_origin(s + 1), 1 - core, 1 - group if far else group),
            (21 if far else 14) + s,
            sibling,
        )

    def own_copy(owner):
        return pltpu.make_async_remote_copy(
            src_ref=k_ref,
            dst_ref=key.at[pl.ds(pl.multiple_of(owner * 2 * half, 2 * half), 2 * half)],
            send_sem=ks_sem.at[28],
            recv_sem=kr_sem.at[28],
            device_id=sibling,
            device_id_type=MESH,
        )

    g_send[:, :grad] = matmul(place_t_ref[...], g_ref[...]).astype(jnp.bfloat16)
    g_send[:, grad:] = matmul(place_t_ref[...], local_ref[...]).astype(jnp.bfloat16)
    pl.semaphore_wait(barrier, n)

    start_all(g_send, g_recv, gs_sem, gr_sem)
    ring_copy(0).start()
    own_copy(me).start()
    g_recv[rows_of(me), :] = g_send[rows_of(me), :]

    @pl.loop(0, tiles)
    def _(t):
        at = pl.ds(pl.multiple_of(t * COLUMNS, COLUMNS), COLUMNS)
        x_send[:, at] = matmul(place_t_ref[...], x_ref[:, at]).astype(jnp.bfloat16)

    start_all(x_send, x_recv, xs_sem, xr_sem)
    key[pl.ds(pl.multiple_of(me * 2 * half, 2 * half), 2 * half), :] = k_ref[...]
    x_recv[rows_of(me), :] = x_send[rows_of(me), :]

    wait_arrivals(g_send, g_recv, gs_sem, gr_sem)
    mask = g_recv[:, grad:].astype(jnp.float32) > 0.5
    reduced[...] = jnp.where(
        mask, adapter_scale * matmul(g_recv[:, :grad], up_ref[...], NT), 0.0
    ).astype(jnp.bfloat16)

    @pl.loop(0, tiles)
    def _(t):
        at = pl.ds(pl.multiple_of(t * COLUMNS, COLUMNS), COLUMNS)
        part[:, at] = matmul(reduced[...], down_ref[at, :], NT).astype(jnp.bfloat16)

    start_all(part, returned, ps_sem, pr_sem)
    returned[rows_of(me), :] = part[rows_of(me), :]

    steps = RING - 1
    for s in range(steps):
        ring_arrival(s).wait_recv()
        if s + 1 < steps:
            ring_copy(s + 1).start()
        across_copy(s).start()
        sibling_copy(s, False).start()
        if s:
            across_arrival(s - 1).wait_recv()
            sibling_copy(s - 1, True).start()

    wait_arrivals(x_send, x_recv, xs_sem, xr_sem)
    h_sum[...] = jnp.zeros_like(h_sum)

    @pl.loop(0, tiles)
    def _(t):
        at = pl.ds(pl.multiple_of(t * COLUMNS, COLUMNS), COLUMNS)
        h_sum[...] += matmul(x_recv[:, at], down_ref[at, :])
        down_grads_ref[at, :] = (gradient_norm * matmul(x_recv[:, at], reduced[...], TN)).astype(
            jnp.bfloat16
        )

    h = jnp.where(mask, h_sum[...], 0.0).astype(jnp.bfloat16)
    up_grads_ref[...] = (adapter_scale * gradient_norm * matmul(h, g_recv[:, :grad], TN)).astype(
        jnp.bfloat16
    )

    across_arrival(steps - 1).wait_recv()
    sibling_copy(steps - 1, True).start()
    own_copy(chip * 2 + 1 - core).wait_recv()
    for s in range(steps):
        sibling_arrival(s, False).wait_recv()
        sibling_arrival(s, True).wait_recv()

    @pl.loop(0, tiles)
    def _(t):
        at = pl.ds(pl.multiple_of(t * COLUMNS, COLUMNS), COLUMNS)
        base[:, at] = matmul(g_ref[...], key[at, :], NT)

    wait_arrivals(part, returned, ps_sem, pr_sem)

    @pl.loop(0, tiles)
    def _(t):
        at = pl.ds(pl.multiple_of(t * COLUMNS, COLUMNS), COLUMNS)
        out_ref[:, at] = (base[:, at] + matmul(place_ref[...], returned[:, at])).astype(jnp.bfloat16)

    wait_sent(g_send, g_recv, gs_sem, gr_sem)
    wait_sent(x_send, x_recv, xs_sem, xr_sem)
    wait_sent(part, returned, ps_sem, pr_sem)
    own_copy(me).wait_send()
    for s in range(steps):
        ring_copy(s).wait_send()
        across_copy(s).wait_send()
        sibling_copy(s, False).wait_send()
        sibling_copy(s, True).wait_send()


def fused_shards(
    token_input_rows,
    output_gradient_rows,
    token_tenant_index,
    tenant_slot_index,
    key_matrix,
    adapter_down_weight,
    adapter_up_weight,
):
    holders = lax.axis_size("owner")
    rows, width = token_input_rows.shape
    grad = output_gradient_rows.shape[1]
    cap = 2 * rows // holders
    total = holders * cap
    held = TEN_DEV * ADAPTER_RANK
    tenants = tenant_slot_index.shape[0]
    named = token_tenant_index[:, None] == jnp.arange(tenants, dtype=jnp.int32)[None, :]
    slot_of = jnp.sum(jnp.where(named, tenant_slot_index[None, :], 0), axis=1)
    target = slot_of // TEN_DEV
    same = target[:, None] == target[None, :]
    before = jnp.arange(rows)[None, :] < jnp.arange(rows)[:, None]
    bucket_place = target * cap + jnp.sum((same & before).astype(jnp.int32), axis=1)
    slots = jnp.arange(total, dtype=jnp.int32)
    place = (bucket_place[:, None] == slots[None, :]).astype(jnp.bfloat16)
    place_t = (bucket_place[None, :] == slots[:, None]).astype(jnp.bfloat16)
    column = jnp.arange(held, dtype=jnp.int32) // ADAPTER_RANK
    local = ((slot_of % TEN_DEV)[:, None] == column[None, :]).astype(jnp.bfloat16)
    vmem = pl.BlockSpec(memory_space=pltpu.VMEM)
    return pl.pallas_call(
        functools.partial(fused_kernel, holders, cap),
        out_shape=(
            jax.ShapeDtypeStruct((rows, width), jnp.bfloat16),
            jax.ShapeDtypeStruct((width, held), jnp.bfloat16),
            jax.ShapeDtypeStruct((held, grad), jnp.bfloat16),
        ),
        in_specs=[vmem] * 8,
        out_specs=(vmem,) * 3,
        scratch_shapes=[
            pltpu.VMEM((total, width), jnp.bfloat16),
            pltpu.VMEM((total, width), jnp.bfloat16),
            pltpu.VMEM((total, grad + held), jnp.bfloat16),
            pltpu.VMEM((total, grad + held), jnp.bfloat16),
            pltpu.VMEM((total, width), jnp.bfloat16),
            pltpu.VMEM((total, width), jnp.bfloat16),
            pltpu.VMEM((width, grad), jnp.bfloat16),
            pltpu.VMEM((rows, width), jnp.float32),
            pltpu.VMEM((total, held), jnp.bfloat16),
            pltpu.VMEM((total, held), jnp.float32),
        ]
        + [pltpu.SemaphoreType.DMA((holders,))] * 6
        + [pltpu.SemaphoreType.DMA((29,))] * 2,
        compiler_params=pltpu.CompilerParams(
            collective_id=0, has_side_effects=True, vmem_limit_bytes=48 * 2**20
        ),
        name="fused_backward",
    )(
        place,
        place_t,
        local,
        token_input_rows,
        output_gradient_rows,
        key_matrix,
        adapter_down_weight,
        adapter_up_weight,
    )


def shards(
    token_input_rows,
    output_gradient_rows,
    token_tenant_index,
    tenant_slot_index,
    key_matrix,
    adapter_down_weight,
    adapter_up_weight,
):
    holders = lax.axis_size("owner")
    row_count = token_input_rows.shape[0]
    feat_width = token_input_rows.shape[1]
    grad_width = output_gradient_rows.shape[1]
    capacity = 2 * row_count // holders
    total_slots = holders * capacity
    slot_of = tenant_slot_index[token_tenant_index]
    target = slot_of // TEN_DEV
    local_index = slot_of % TEN_DEV
    onehot = (target[:, None] == jnp.arange(holders, dtype=jnp.int32)[None, :]).astype(jnp.int32)
    earlier = jnp.cumsum(onehot, axis=0) - onehot
    bucket_place = target * capacity + jnp.sum(earlier * onehot, axis=1)
    send_x = (
        jnp.zeros((total_slots, feat_width), jnp.bfloat16)
        .at[bucket_place]
        .set(token_input_rows)
        .reshape(holders, capacity, feat_width)
    )
    send_g = (
        jnp.zeros((total_slots, grad_width), jnp.bfloat16)
        .at[bucket_place]
        .set(output_gradient_rows)
        .reshape(holders, capacity, grad_width)
    )
    send_id = (
        jnp.full((total_slots,), -1, jnp.int32)
        .at[bucket_place]
        .set(local_index)
        .reshape(holders, capacity)
    )
    received_input, received_gradient, received_tenant = (
        lax.all_to_all(send_x, "owner", split_axis=0, concat_axis=0, tiled=True),
        lax.all_to_all(send_g, "owner", split_axis=0, concat_axis=0, tiled=True),
        lax.all_to_all(send_id, "owner", split_axis=0, concat_axis=0, tiled=True),
    )
    adapter_part, down_grads, up_grads = slot_holder_products(
        received_input.reshape(total_slots, feat_width),
        received_gradient.reshape(total_slots, grad_width),
        received_tenant.reshape(total_slots),
        adapter_down_weight,
        adapter_up_weight,
    )
    returned = lax.all_to_all(
        adapter_part.reshape(holders, capacity, feat_width),
        "owner",
        split_axis=0,
        concat_axis=0,
        tiled=True,
    )
    mine = returned.reshape(total_slots, feat_width)[bucket_place]
    base = frozen_product(output_gradient_rows, key_matrix)
    input_grads = (base + mine.astype(jnp.float32)).astype(jnp.bfloat16)
    return (input_grads, down_grads, up_grads)


def solution(mesh):
    on_grid = mesh.shape["groups"] == 2 and mesh.shape["owner"] == 2 * RING
    return jax.shard_map(
        fused_shards if on_grid else shards,
        mesh=mesh,
        in_specs=(
            P(("groups", "owner"), None),
            P(("groups", "owner"), None),
            P(("groups", "owner")),
            P("groups"),
            P("owner", None),
            P(None, ("groups", "owner")),
            P(("groups", "owner"), None),
        ),
        out_specs=(
            P(("groups", "owner"), None),
            P(None, ("groups", "owner")),
            P(("groups", "owner"), None),
        ),
        check_vma=False,
    )
```

```python
import functools

import jax
import jax.numpy as jnp
from jax import lax
from jax.experimental import pallas as pl
from jax.experimental.pallas import tpu as pltpu
from jax.sharding import PartitionSpec as P

ADAPTER_RANK = 64
TEN_DEV = 2


adapter_scale = 2.0
gradient_norm = 1.0 / 64.0


def slot_holder_products(
    received_input, received_gradient, received_tenant, adapter_down_weight, adapter_up_weight
):
    column_tenant = jnp.arange(TEN_DEV * ADAPTER_RANK, dtype=jnp.int32) // ADAPTER_RANK
    valid_mask = received_tenant[:, None] == column_tenant[None, :]
    reduced_input = jnp.where(
        valid_mask,
        jnp.dot(received_input, adapter_down_weight, preferred_element_type=jnp.float32),
        0.0,
    ).astype(jnp.bfloat16)
    backward_pass = lax.dot_general(
        received_gradient,
        adapter_up_weight,
        (((1,), (1,)), ((), ())),
        preferred_element_type=jnp.float32,
    )
    reduced_gradient = jnp.where(valid_mask, adapter_scale * backward_pass, 0.0).astype(
        jnp.bfloat16
    )
    down_grads = (
        gradient_norm
        * lax.dot_general(
            received_input,
            reduced_gradient,
            (((0,), (0,)), ((), ())),
            preferred_element_type=jnp.float32,
        )
    ).astype(jnp.bfloat16)
    up_grads = (
        adapter_scale
        * gradient_norm
        * lax.dot_general(
            reduced_input,
            received_gradient,
            (((0,), (0,)), ((), ())),
            preferred_element_type=jnp.float32,
        )
    ).astype(jnp.bfloat16)
    adapter_part = lax.dot_general(
        reduced_gradient,
        adapter_down_weight,
        (((1,), (1,)), ((), ())),
        preferred_element_type=jnp.float32,
    ).astype(jnp.bfloat16)
    return (adapter_part, down_grads, up_grads)


def frozen_product(output_gradient_rows, key_matrix):
    return lax.dot_general(
        output_gradient_rows,
        lax.all_gather(key_matrix, "owner", axis=0, tiled=True),
        (((1,), (1,)), ((), ())),
        preferred_element_type=jnp.float32,
    )


MESH = pl.DeviceIdType.MESH
NT = (((1,), (1,)), ((), ()))
TN = (((0,), (0,)), ((), ()))
COLUMNS = 512
AHEAD = 2
EACH = 2
RING = 8


def matmul(a, b, dims=(((1,), (0,)), ((), ()))):
    return lax.dot_general(a, b, dims, preferred_element_type=jnp.float32)


def ring_chip(position):
    up = (position < 4).astype(jnp.int32)
    z = up * position + (1 - up) * (7 - position)
    return z * 2 + (1 - up)


def fused_kernel(
    n,
    cap,
    place_ref,
    place_t_ref,
    local_ref,
    x_hbm,
    g_hbm,
    k_hbm,
    down_hbm,
    up_hbm,
    out_ref,
    down_grads_ref,
    up_grads_ref,
    x_send,
    x_recv,
    g_send,
    g_recv,
    part,
    returned,
    key,
    base,
    reduced,
    h_sum,
    x_ref,
    g_ref,
    k_ref,
    down_ref,
    up_ref,
    in_sem,
    gs_sem,
    gr_sem,
    xs_sem,
    xr_sem,
    ps_sem,
    pr_sem,
    ks_sem,
    kr_sem,
):
    group = lax.axis_index("groups")
    me = lax.axis_index("owner")
    width = x_ref.shape[1]
    grad = g_ref.shape[1]
    tiles = width // COLUMNS
    core = me % 2
    chip = me // 2
    z, x = chip // 2, chip % 2
    position = (1 - x) * z + x * (7 - z)
    step_by = 1 - 2 * core
    sibling = (group, chip * 2 + 1 - core)
    across = (1 - group, me)
    ahead = (group, ring_chip((position + step_by + RING) % RING) * 2 + core)

    loads = [
        pltpu.make_async_copy(src, dst, in_sem.at[i])
        for i, (src, dst) in enumerate(
            [
                (g_hbm, g_ref),
                (k_hbm, k_ref),
                (x_hbm, x_ref),
                (up_hbm, up_ref),
                (down_hbm, down_ref),
            ]
        )
    ]
    for load in loads:
        load.start()

    barrier = pltpu.get_barrier_semaphore()

    @pl.loop(1, n)
    def _(i):
        pl.semaphore_signal(barrier, inc=1, device_id=(group, (me + i) % n), device_id_type=MESH)

    pl.semaphore_signal(barrier, inc=1, device_id=across, device_id_type=MESH)

    def rows_of(owner):
        return pl.ds(pl.multiple_of(owner * cap, cap), cap)

    def row_copy(src, dst, send, recv, at, owner, i):
        return pltpu.make_async_remote_copy(
            src_ref=src.at[rows_of(owner)],
            dst_ref=dst.at[rows_of(at)],
            send_sem=send.at[i],
            recv_sem=recv.at[i],
            device_id=(group, owner),
            device_id_type=MESH,
        )

    def start_all(src, dst, send, recv):
        @pl.loop(1, n)
        def _(i):
            row_copy(src, dst, send, recv, me, (me + i) % n, i).start()

    def wait_arrivals(src, dst, send, recv):
        @pl.loop(1, n)
        def _(i):
            row_copy(src, dst, send, recv, (me + n - i) % n, (me + i) % n, i).wait_recv()

    def wait_sent(src, dst, send, recv):
        @pl.loop(1, n)
        def _(i):
            row_copy(src, dst, send, recv, me, (me + i) % n, i).wait_send()

    half = k_ref.shape[0] // 2

    def key_rows(at_position, of_core, of_half):
        owner = ring_chip(at_position) * 2 + of_core
        return pl.ds(pl.multiple_of((owner * 2 + of_half) * half, half), half)

    def key_copy(rows, sem, device, src=None):
        return pltpu.make_async_remote_copy(
            src_ref=key.at[rows] if src is None else src,
            dst_ref=key.at[rows],
            send_sem=ks_sem.at[sem],
            recv_sem=kr_sem.at[sem],
            device_id=device,
            device_id_type=MESH,
        )

    def origin(s):
        return (position + (RING - s) * step_by + 2 * RING * RING) % RING

    def sibling_origin(s):
        return (position - (RING - s) * step_by + 2 * RING * RING) % RING

    def ring_copy(s):
        if s == 0:
            return key_copy(
                key_rows(position, core, group),
                0,
                ahead,
                k_ref.at[pl.ds(pl.multiple_of(group * half, half), half)],
            )
        return key_copy(key_rows(origin(s), core, group), s, ahead)

    def ring_arrival(s):
        return key_copy(key_rows(origin(s + 1), core, group), s, ahead)

    def across_copy(s):
        return key_copy(key_rows(origin(s + 1), core, group), 7 + s, across)

    def across_arrival(s):
        return key_copy(key_rows(origin(s + 1), core, 1 - group), 7 + s, across)

    def sibling_copy(s, far):
        return key_copy(
            key_rows(origin(s + 1), core, 1 - group if far else group), (21 if far else 14) + s, sibling
        )

    def sibling_arrival(s, far):
        return key_copy(
            key_rows(sibling_origin(s + 1), 1 - core, 1 - group if far else group),
            (21 if far else 14) + s,
            sibling,
        )

    def own_copy(owner):
        return pltpu.make_async_remote_copy(
            src_ref=k_ref,
            dst_ref=key.at[pl.ds(pl.multiple_of(owner * 2 * half, 2 * half), 2 * half)],
            send_sem=ks_sem.at[28],
            recv_sem=kr_sem.at[28],
            device_id=sibling,
            device_id_type=MESH,
        )

    loads[0].wait()
    g_send[:, :grad] = matmul(place_t_ref[...], g_ref[...]).astype(jnp.bfloat16)
    g_send[:, grad:] = matmul(place_t_ref[...], local_ref[...]).astype(jnp.bfloat16)
    pl.semaphore_wait(barrier, n)

    start_all(g_send, g_recv, gs_sem, gr_sem)
    loads[1].wait()
    ring_copy(0).start()
    own_copy(me).start()
    g_recv[rows_of(me), :] = g_send[rows_of(me), :]
    loads[2].wait()

    @pl.loop(0, tiles)
    def _(t):
        at = pl.ds(pl.multiple_of(t * COLUMNS, COLUMNS), COLUMNS)
        x_send[:, at] = matmul(place_t_ref[...], x_ref[:, at]).astype(jnp.bfloat16)

    x_queue = [(x_send, x_recv, xs_sem, xr_sem, i) for i in range(1, n)]
    part_queue = [(part, returned, ps_sem, pr_sem, i) for i in range(1, n)]
    queue = x_queue + part_queue

    def start_some(count):
        for _ in range(min(count, len(queue))):
            src, dst, send, recv, i = queue.pop(0)
            row_copy(src, dst, send, recv, me, (me + i) % n, i).start()

    start_some(AHEAD)
    key[pl.ds(pl.multiple_of(me * 2 * half, 2 * half), 2 * half), :] = k_ref[...]
    x_recv[rows_of(me), :] = x_send[rows_of(me), :]

    wait_arrivals(g_send, g_recv, gs_sem, gr_sem)
    loads[3].wait()
    mask = g_recv[:, grad:].astype(jnp.float32) > 0.5
    reduced[...] = jnp.where(
        mask, adapter_scale * matmul(g_recv[:, :grad], up_ref[...], NT), 0.0
    ).astype(jnp.bfloat16)
    loads[4].wait()

    @pl.loop(0, tiles)
    def _(t):
        at = pl.ds(pl.multiple_of(t * COLUMNS, COLUMNS), COLUMNS)
        part[:, at] = matmul(reduced[...], down_ref[at, :], NT).astype(jnp.bfloat16)

    returned[rows_of(me), :] = part[rows_of(me), :]

    steps = RING - 1
    for s in range(steps):
        ring_arrival(s).wait_recv()
        if s + 1 < steps:
            ring_copy(s + 1).start()
        across_copy(s).start()
        sibling_copy(s, False).start()
        if s:
            across_arrival(s - 1).wait_recv()
            sibling_copy(s - 1, True).start()
        start_some(EACH)
    start_some(2 * n)

    wait_arrivals(x_send, x_recv, xs_sem, xr_sem)
    h_sum[...] = jnp.zeros_like(h_sum)

    @pl.loop(0, tiles)
    def _(t):
        at = pl.ds(pl.multiple_of(t * COLUMNS, COLUMNS), COLUMNS)
        h_sum[...] += matmul(x_recv[:, at], down_ref[at, :])
        down_grads_ref[at, :] = (gradient_norm * matmul(x_recv[:, at], reduced[...], TN)).astype(
            jnp.bfloat16
        )

    h = jnp.where(mask, h_sum[...], 0.0).astype(jnp.bfloat16)
    up_grads_ref[...] = (adapter_scale * gradient_norm * matmul(h, g_recv[:, :grad], TN)).astype(
        jnp.bfloat16
    )

    across_arrival(steps - 1).wait_recv()
    sibling_copy(steps - 1, True).start()
    own_copy(chip * 2 + 1 - core).wait_recv()
    for s in range(steps):
        sibling_arrival(s, False).wait_recv()
        sibling_arrival(s, True).wait_recv()

    @pl.loop(0, tiles)
    def _(t):
        at = pl.ds(pl.multiple_of(t * COLUMNS, COLUMNS), COLUMNS)
        base[:, at] = matmul(g_ref[...], key[at, :], NT)

    wait_arrivals(part, returned, ps_sem, pr_sem)

    @pl.loop(0, tiles)
    def _(t):
        at = pl.ds(pl.multiple_of(t * COLUMNS, COLUMNS), COLUMNS)
        out_ref[:, at] = (base[:, at] + matmul(place_ref[...], returned[:, at])).astype(jnp.bfloat16)

    wait_sent(g_send, g_recv, gs_sem, gr_sem)
    wait_sent(x_send, x_recv, xs_sem, xr_sem)
    wait_sent(part, returned, ps_sem, pr_sem)
    own_copy(me).wait_send()
    for s in range(steps):
        ring_copy(s).wait_send()
        across_copy(s).wait_send()
        sibling_copy(s, False).wait_send()
        sibling_copy(s, True).wait_send()


def fused_shards(
    token_input_rows,
    output_gradient_rows,
    token_tenant_index,
    tenant_slot_index,
    key_matrix,
    adapter_down_weight,
    adapter_up_weight,
):
    holders = lax.axis_size("owner")
    rows, width = token_input_rows.shape
    grad = output_gradient_rows.shape[1]
    cap = 2 * rows // holders
    total = holders * cap
    held = TEN_DEV * ADAPTER_RANK
    tenants = tenant_slot_index.shape[0]
    named = token_tenant_index[:, None] == jnp.arange(tenants, dtype=jnp.int32)[None, :]
    slot_of = jnp.sum(jnp.where(named, tenant_slot_index[None, :], 0), axis=1)
    target = slot_of // TEN_DEV
    same = target[:, None] == target[None, :]
    before = jnp.arange(rows)[None, :] < jnp.arange(rows)[:, None]
    bucket_place = target * cap + jnp.sum((same & before).astype(jnp.int32), axis=1)
    slots = jnp.arange(total, dtype=jnp.int32)
    place = (bucket_place[:, None] == slots[None, :]).astype(jnp.bfloat16)
    place_t = (bucket_place[None, :] == slots[:, None]).astype(jnp.bfloat16)
    column = jnp.arange(held, dtype=jnp.int32) // ADAPTER_RANK
    local = ((slot_of % TEN_DEV)[:, None] == column[None, :]).astype(jnp.bfloat16)
    vmem = pl.BlockSpec(memory_space=pltpu.VMEM)
    return pl.pallas_call(
        functools.partial(fused_kernel, holders, cap),
        out_shape=(
            jax.ShapeDtypeStruct((rows, width), jnp.bfloat16),
            jax.ShapeDtypeStruct((width, held), jnp.bfloat16),
            jax.ShapeDtypeStruct((held, grad), jnp.bfloat16),
        ),
        in_specs=[vmem] * 3 + [pl.BlockSpec(memory_space=pl.ANY)] * 5,
        out_specs=(vmem,) * 3,
        scratch_shapes=[
            pltpu.VMEM((total, width), jnp.bfloat16),
            pltpu.VMEM((total, width), jnp.bfloat16),
            pltpu.VMEM((total, grad + held), jnp.bfloat16),
            pltpu.VMEM((total, grad + held), jnp.bfloat16),
            pltpu.VMEM((total, width), jnp.bfloat16),
            pltpu.VMEM((total, width), jnp.bfloat16),
            pltpu.VMEM((width, grad), jnp.bfloat16),
            pltpu.VMEM((rows, width), jnp.float32),
            pltpu.VMEM((total, held), jnp.bfloat16),
            pltpu.VMEM((total, held), jnp.float32),
            pltpu.VMEM((rows, width), jnp.bfloat16),
            pltpu.VMEM((rows, grad), jnp.bfloat16),
            pltpu.VMEM(key_matrix.shape, jnp.bfloat16),
            pltpu.VMEM((width, held), jnp.bfloat16),
            pltpu.VMEM((held, grad), jnp.bfloat16),
            pltpu.SemaphoreType.DMA((5,)),
        ]
        + [pltpu.SemaphoreType.DMA((holders,))] * 6
        + [pltpu.SemaphoreType.DMA((29,))] * 2,
        compiler_params=pltpu.CompilerParams(
            collective_id=0, has_side_effects=True, vmem_limit_bytes=48 * 2**20
        ),
        name="fused_backward",
    )(
        place,
        place_t,
        local,
        token_input_rows,
        output_gradient_rows,
        key_matrix,
        adapter_down_weight,
        adapter_up_weight,
    )


def shards(
    token_input_rows,
    output_gradient_rows,
    token_tenant_index,
    tenant_slot_index,
    key_matrix,
    adapter_down_weight,
    adapter_up_weight,
):
    holders = lax.axis_size("owner")
    row_count = token_input_rows.shape[0]
    feat_width = token_input_rows.shape[1]
    grad_width = output_gradient_rows.shape[1]
    capacity = 2 * row_count // holders
    total_slots = holders * capacity
    slot_of = tenant_slot_index[token_tenant_index]
    target = slot_of // TEN_DEV
    local_index = slot_of % TEN_DEV
    onehot = (target[:, None] == jnp.arange(holders, dtype=jnp.int32)[None, :]).astype(jnp.int32)
    earlier = jnp.cumsum(onehot, axis=0) - onehot
    bucket_place = target * capacity + jnp.sum(earlier * onehot, axis=1)
    send_x = (
        jnp.zeros((total_slots, feat_width), jnp.bfloat16)
        .at[bucket_place]
        .set(token_input_rows)
        .reshape(holders, capacity, feat_width)
    )
    send_g = (
        jnp.zeros((total_slots, grad_width), jnp.bfloat16)
        .at[bucket_place]
        .set(output_gradient_rows)
        .reshape(holders, capacity, grad_width)
    )
    send_id = (
        jnp.full((total_slots,), -1, jnp.int32)
        .at[bucket_place]
        .set(local_index)
        .reshape(holders, capacity)
    )
    received_input, received_gradient, received_tenant = (
        lax.all_to_all(send_x, "owner", split_axis=0, concat_axis=0, tiled=True),
        lax.all_to_all(send_g, "owner", split_axis=0, concat_axis=0, tiled=True),
        lax.all_to_all(send_id, "owner", split_axis=0, concat_axis=0, tiled=True),
    )
    adapter_part, down_grads, up_grads = slot_holder_products(
        received_input.reshape(total_slots, feat_width),
        received_gradient.reshape(total_slots, grad_width),
        received_tenant.reshape(total_slots),
        adapter_down_weight,
        adapter_up_weight,
    )
    returned = lax.all_to_all(
        adapter_part.reshape(holders, capacity, feat_width),
        "owner",
        split_axis=0,
        concat_axis=0,
        tiled=True,
    )
    mine = returned.reshape(total_slots, feat_width)[bucket_place]
    base = frozen_product(output_gradient_rows, key_matrix)
    input_grads = (base + mine.astype(jnp.float32)).astype(jnp.bfloat16)
    return (input_grads, down_grads, up_grads)


def solution(mesh):
    on_grid = mesh.shape["groups"] == 2 and mesh.shape["owner"] == 2 * RING
    return jax.shard_map(
        fused_shards if on_grid else shards,
        mesh=mesh,
        in_specs=(
            P(("groups", "owner"), None),
            P(("groups", "owner"), None),
            P(("groups", "owner")),
            P("groups"),
            P("owner", None),
            P(None, ("groups", "owner")),
            P(("groups", "owner"), None),
        ),
        out_specs=(
            P(("groups", "owner"), None),
            P(None, ("groups", "owner")),
            P(("groups", "owner"), None),
        ),
        check_vma=False,
    )
```

```python
import functools

import jax
import jax.numpy as jnp
from jax import lax
from jax.experimental import pallas as pl
from jax.experimental.pallas import tpu as pltpu
from jax.sharding import PartitionSpec as P

ADAPTER_RANK = 64
TEN_DEV = 2


adapter_scale = 2.0
gradient_norm = 1.0 / 64.0


def slot_holder_products(
    received_input, received_gradient, received_tenant, adapter_down_weight, adapter_up_weight
):
    column_tenant = jnp.arange(TEN_DEV * ADAPTER_RANK, dtype=jnp.int32) // ADAPTER_RANK
    valid_mask = received_tenant[:, None] == column_tenant[None, :]
    reduced_input = jnp.where(
        valid_mask,
        jnp.dot(received_input, adapter_down_weight, preferred_element_type=jnp.float32),
        0.0,
    ).astype(jnp.bfloat16)
    backward_pass = lax.dot_general(
        received_gradient,
        adapter_up_weight,
        (((1,), (1,)), ((), ())),
        preferred_element_type=jnp.float32,
    )
    reduced_gradient = jnp.where(valid_mask, adapter_scale * backward_pass, 0.0).astype(
        jnp.bfloat16
    )
    down_grads = (
        gradient_norm
        * lax.dot_general(
            received_input,
            reduced_gradient,
            (((0,), (0,)), ((), ())),
            preferred_element_type=jnp.float32,
        )
    ).astype(jnp.bfloat16)
    up_grads = (
        adapter_scale
        * gradient_norm
        * lax.dot_general(
            reduced_input,
            received_gradient,
            (((0,), (0,)), ((), ())),
            preferred_element_type=jnp.float32,
        )
    ).astype(jnp.bfloat16)
    adapter_part = lax.dot_general(
        reduced_gradient,
        adapter_down_weight,
        (((1,), (1,)), ((), ())),
        preferred_element_type=jnp.float32,
    ).astype(jnp.bfloat16)
    return (adapter_part, down_grads, up_grads)


def frozen_product(output_gradient_rows, key_matrix):
    return lax.dot_general(
        output_gradient_rows,
        lax.all_gather(key_matrix, "owner", axis=0, tiled=True),
        (((1,), (1,)), ((), ())),
        preferred_element_type=jnp.float32,
    )


MESH = pl.DeviceIdType.MESH
NT = (((1,), (1,)), ((), ()))
TN = (((0,), (0,)), ((), ()))
COLUMNS = 512
AHEAD = 8
EACH = 2
LAYERS = 4


def matmul(a, b, dims=(((1,), (0,)), ((), ()))):
    return lax.dot_general(a, b, dims, preferred_element_type=jnp.float32)


def fused_kernel(
    n,
    cap,
    place_ref,
    place_t_ref,
    local_ref,
    x_hbm,
    g_hbm,
    k_hbm,
    down_hbm,
    up_hbm,
    out_ref,
    down_grads_ref,
    up_grads_ref,
    x_send,
    x_recv,
    g_send,
    g_recv,
    part,
    returned,
    key,
    base,
    reduced,
    h_sum,
    x_ref,
    g_ref,
    k_ref,
    down_ref,
    up_ref,
    in_sem,
    gs_sem,
    gr_sem,
    xs_sem,
    xr_sem,
    ps_sem,
    pr_sem,
    ks_sem,
    kr_sem,
):
    group = lax.axis_index("groups")
    me = lax.axis_index("owner")
    width = x_ref.shape[1]
    grad = g_ref.shape[1]
    tiles = width // COLUMNS
    core = me % 2
    chip = me // 2
    z, x = chip // 2, chip % 2
    sibling = (group, chip * 2 + 1 - core)
    across = (1 - group, me)
    beside = (group, (z * 2 + 1 - x) * 2 + core)

    loads = [
        pltpu.make_async_copy(src, dst, in_sem.at[i])
        for i, (src, dst) in enumerate(
            [
                (g_hbm, g_ref),
                (k_hbm, k_ref),
                (x_hbm, x_ref),
                (up_hbm, up_ref),
                (down_hbm, down_ref),
            ]
        )
    ]
    for load in loads:
        load.start()

    barrier = pltpu.get_barrier_semaphore()

    @pl.loop(1, n)
    def _(i):
        pl.semaphore_signal(barrier, inc=1, device_id=(group, (me + i) % n), device_id_type=MESH)

    pl.semaphore_signal(barrier, inc=1, device_id=across, device_id_type=MESH)

    def rows_of(owner):
        return pl.ds(pl.multiple_of(owner * cap, cap), cap)

    def row_copy(src, dst, send, recv, at, owner, i):
        return pltpu.make_async_remote_copy(
            src_ref=src.at[rows_of(owner)],
            dst_ref=dst.at[rows_of(at)],
            send_sem=send.at[i],
            recv_sem=recv.at[i],
            device_id=(group, owner),
            device_id_type=MESH,
        )

    def start_all(src, dst, send, recv):
        @pl.loop(1, n)
        def _(i):
            row_copy(src, dst, send, recv, me, (me + i) % n, i).start()

    def wait_arrivals(src, dst, send, recv):
        @pl.loop(1, n)
        def _(i):
            row_copy(src, dst, send, recv, (me + n - i) % n, (me + i) % n, i).wait_recv()

    def wait_sent(src, dst, send, recv):
        @pl.loop(1, n)
        def _(i):
            row_copy(src, dst, send, recv, me, (me + i) % n, i).wait_send()

    half = k_ref.shape[0] // 2

    def key_rows(of_z, of_x, of_core, of_half):
        owner = (of_z * 2 + of_x) * 2 + of_core
        return pl.ds(pl.multiple_of((owner * 2 + of_half) * half, half), half)

    def key_copy(rows, sent, landed, device, own=False):
        src = k_ref.at[pl.ds(pl.multiple_of(group * half, half), half)] if own else key.at[rows]
        return pltpu.make_async_remote_copy(
            src_ref=src,
            dst_ref=key.at[rows],
            send_sem=ks_sem.at[sent],
            recv_sem=kr_sem.at[landed],
            device_id=device,
            device_id_type=MESH,
        )

    def z_copy(of_z, up, own=False):
        device = (group, ((z + 1 if up else z - 1) * 2 + x) * 2 + core)
        rows = key_rows(of_z, x, core, group)
        return key_copy(rows, of_z if up else 4 + of_z, of_z, device, own)

    def z_arrival(of_z):
        return key_copy(key_rows(of_z, x, core, group), of_z, of_z, beside)

    def x_copy(of_z, own=False):
        return key_copy(key_rows(of_z, x, core, group), 8 + of_z, 8 + of_z, beside, own)

    def x_arrival(of_z):
        return key_copy(key_rows(of_z, 1 - x, core, group), 8 + of_z, 8 + of_z, beside)

    def y_copy(of_z, of_x):
        sem = 16 + of_z * 2 + of_x
        return key_copy(key_rows(of_z, of_x, core, group), sem, sem, across)

    def y_arrival(of_z, of_x):
        sem = 16 + of_z * 2 + of_x
        return key_copy(key_rows(of_z, of_x, core, 1 - group), sem, sem, across)

    def sibling_copy(of_z, of_x, far, of_core=core):
        sem = 24 + (of_z * 2 + of_x) * 2 + far
        rows = key_rows(of_z, of_x, of_core, 1 - group if far else group)
        return key_copy(rows, sem, sem, sibling)

    def sibling_arrival(of_z, of_x, far):
        return sibling_copy(of_z, of_x, far, 1 - core)

    def hand_on(of_z, up):
        z_arrival(of_z).wait_recv()

        @pl.when(z < LAYERS - 1 if up else z > 0)
        def _():
            z_copy(of_z, up).start()

        x_copy(of_z).start()
        y_copy(of_z, x).start()
        sibling_copy(of_z, x, 0).start()

    def own_copy(owner):
        return pltpu.make_async_remote_copy(
            src_ref=k_ref,
            dst_ref=key.at[pl.ds(pl.multiple_of(owner * 2 * half, 2 * half), 2 * half)],
            send_sem=ks_sem.at[40],
            recv_sem=kr_sem.at[40],
            device_id=sibling,
            device_id_type=MESH,
        )

    loads[0].wait()
    g_send[:, :grad] = matmul(place_t_ref[...], g_ref[...]).astype(jnp.bfloat16)
    g_send[:, grad:] = matmul(place_t_ref[...], local_ref[...]).astype(jnp.bfloat16)
    pl.semaphore_wait(barrier, n)

    start_all(g_send, g_recv, gs_sem, gr_sem)
    loads[1].wait()

    @pl.when(z < LAYERS - 1)
    def _():
        z_copy(z, True, own=True).start()

    @pl.when(z > 0)
    def _():
        z_copy(z, False, own=True).start()

    x_copy(z, own=True).start()
    own_copy(me).start()
    g_recv[rows_of(me), :] = g_send[rows_of(me), :]
    loads[2].wait()

    @pl.loop(0, tiles)
    def _(t):
        at = pl.ds(pl.multiple_of(t * COLUMNS, COLUMNS), COLUMNS)
        x_send[:, at] = matmul(place_t_ref[...], x_ref[:, at]).astype(jnp.bfloat16)

    far_first = sorted(range(1, n), key=lambda i: abs(i - n // 2))
    x_queue = [(x_send, x_recv, xs_sem, xr_sem, i) for i in far_first]
    part_queue = [(part, returned, ps_sem, pr_sem, i) for i in far_first]
    queue = x_queue + part_queue

    def start_some(count):
        for _ in range(min(count, len(queue))):
            src, dst, send, recv, i = queue.pop(0)
            row_copy(src, dst, send, recv, me, (me + i) % n, i).start()

    start_some(AHEAD)
    key[pl.ds(pl.multiple_of(me * 2 * half, 2 * half), 2 * half), :] = k_ref[...]
    x_recv[rows_of(me), :] = x_send[rows_of(me), :]

    wait_arrivals(g_send, g_recv, gs_sem, gr_sem)
    loads[3].wait()
    mask = g_recv[:, grad:].astype(jnp.float32) > 0.5
    reduced[...] = jnp.where(
        mask, adapter_scale * matmul(g_recv[:, :grad], up_ref[...], NT), 0.0
    ).astype(jnp.bfloat16)
    loads[4].wait()

    @pl.loop(0, tiles)
    def _(t):
        at = pl.ds(pl.multiple_of(t * COLUMNS, COLUMNS), COLUMNS)
        part[:, at] = matmul(reduced[...], down_ref[at, :], NT).astype(jnp.bfloat16)

    returned[rows_of(me), :] = part[rows_of(me), :]

    for d in range(1, LAYERS):

        @pl.when(z >= d)
        def _():
            hand_on(z - d, True)

        @pl.when(z + d < LAYERS)
        def _():
            hand_on(z + d, False)

        start_some(EACH)
    layers = [(z + d) % LAYERS for d in range(LAYERS)]
    for of_z in layers:
        x_arrival(of_z).wait_recv()
        y_copy(of_z, 1 - x).start()
        sibling_copy(of_z, 1 - x, 0).start()
        start_some(EACH)
    others = [(of_z, x) for of_z in layers[1:]] + [(of_z, 1 - x) for of_z in layers]
    for chip_at in others:
        y_arrival(*chip_at).wait_recv()
        sibling_copy(*chip_at, 1).start()
        start_some(EACH)
    start_some(2 * n)

    wait_arrivals(x_send, x_recv, xs_sem, xr_sem)
    h_sum[...] = jnp.zeros_like(h_sum)

    @pl.loop(0, tiles)
    def _(t):
        at = pl.ds(pl.multiple_of(t * COLUMNS, COLUMNS), COLUMNS)
        h_sum[...] += matmul(x_recv[:, at], down_ref[at, :])
        down_grads_ref[at, :] = (gradient_norm * matmul(x_recv[:, at], reduced[...], TN)).astype(
            jnp.bfloat16
        )

    h = jnp.where(mask, h_sum[...], 0.0).astype(jnp.bfloat16)
    up_grads_ref[...] = (adapter_scale * gradient_norm * matmul(h, g_recv[:, :grad], TN)).astype(
        jnp.bfloat16
    )

    own_copy(chip * 2 + 1 - core).wait_recv()
    for chip_at in others:
        sibling_arrival(*chip_at, 0).wait_recv()
        sibling_arrival(*chip_at, 1).wait_recv()

    @pl.loop(0, tiles)
    def _(t):
        at = pl.ds(pl.multiple_of(t * COLUMNS, COLUMNS), COLUMNS)
        base[:, at] = matmul(g_ref[...], key[at, :], NT)

    wait_arrivals(part, returned, ps_sem, pr_sem)

    @pl.loop(0, tiles)
    def _(t):
        at = pl.ds(pl.multiple_of(t * COLUMNS, COLUMNS), COLUMNS)
        out_ref[:, at] = (base[:, at] + matmul(place_ref[...], returned[:, at])).astype(jnp.bfloat16)

    wait_sent(g_send, g_recv, gs_sem, gr_sem)
    wait_sent(x_send, x_recv, xs_sem, xr_sem)
    wait_sent(part, returned, ps_sem, pr_sem)
    own_copy(me).wait_send()

    @pl.when(z < LAYERS - 1)
    def _():
        z_copy(z, True, own=True).wait_send()

    @pl.when(z > 0)
    def _():
        z_copy(z, False, own=True).wait_send()

    x_copy(z, own=True).wait_send()
    for d in range(1, LAYERS):

        @pl.when((z >= d) & (z < LAYERS - 1))
        def _():
            z_copy(z - d, True).wait_send()

        @pl.when((z + d < LAYERS) & (z > 0))
        def _():
            z_copy(z + d, False).wait_send()

    for of_z in layers[1:]:
        x_copy(of_z).wait_send()
    for chip_at in others:
        y_copy(*chip_at).wait_send()
        sibling_copy(*chip_at, 0).wait_send()
        sibling_copy(*chip_at, 1).wait_send()


def fused_shards(
    token_input_rows,
    output_gradient_rows,
    token_tenant_index,
    tenant_slot_index,
    key_matrix,
    adapter_down_weight,
    adapter_up_weight,
):
    holders = lax.axis_size("owner")
    rows, width = token_input_rows.shape
    grad = output_gradient_rows.shape[1]
    cap = 2 * rows // holders
    total = holders * cap
    held = TEN_DEV * ADAPTER_RANK
    tenants = tenant_slot_index.shape[0]
    named = token_tenant_index[:, None] == jnp.arange(tenants, dtype=jnp.int32)[None, :]
    slot_of = jnp.sum(jnp.where(named, tenant_slot_index[None, :], 0), axis=1)
    target = slot_of // TEN_DEV
    same = target[:, None] == target[None, :]
    before = jnp.arange(rows)[None, :] < jnp.arange(rows)[:, None]
    bucket_place = target * cap + jnp.sum((same & before).astype(jnp.int32), axis=1)
    slots = jnp.arange(total, dtype=jnp.int32)
    place = (bucket_place[:, None] == slots[None, :]).astype(jnp.bfloat16)
    place_t = (bucket_place[None, :] == slots[:, None]).astype(jnp.bfloat16)
    column = jnp.arange(held, dtype=jnp.int32) // ADAPTER_RANK
    local = ((slot_of % TEN_DEV)[:, None] == column[None, :]).astype(jnp.bfloat16)
    vmem = pl.BlockSpec(memory_space=pltpu.VMEM)
    return pl.pallas_call(
        functools.partial(fused_kernel, holders, cap),
        out_shape=(
            jax.ShapeDtypeStruct((rows, width), jnp.bfloat16),
            jax.ShapeDtypeStruct((width, held), jnp.bfloat16),
            jax.ShapeDtypeStruct((held, grad), jnp.bfloat16),
        ),
        in_specs=[vmem] * 3 + [pl.BlockSpec(memory_space=pltpu.HBM)] * 5,
        out_specs=(vmem,) * 3,
        scratch_shapes=[
            pltpu.VMEM((total, width), jnp.bfloat16),
            pltpu.VMEM((total, width), jnp.bfloat16),
            pltpu.VMEM((total, grad + held), jnp.bfloat16),
            pltpu.VMEM((total, grad + held), jnp.bfloat16),
            pltpu.VMEM((total, width), jnp.bfloat16),
            pltpu.VMEM((total, width), jnp.bfloat16),
            pltpu.VMEM((width, grad), jnp.bfloat16),
            pltpu.VMEM((rows, width), jnp.float32),
            pltpu.VMEM((total, held), jnp.bfloat16),
            pltpu.VMEM((total, held), jnp.float32),
            pltpu.VMEM((rows, width), jnp.bfloat16),
            pltpu.VMEM((rows, grad), jnp.bfloat16),
            pltpu.VMEM(key_matrix.shape, jnp.bfloat16),
            pltpu.VMEM((width, held), jnp.bfloat16),
            pltpu.VMEM((held, grad), jnp.bfloat16),
            pltpu.SemaphoreType.DMA((5,)),
        ]
        + [pltpu.SemaphoreType.DMA((holders,))] * 6
        + [pltpu.SemaphoreType.DMA((41,))] * 2,
        compiler_params=pltpu.CompilerParams(
            collective_id=0, has_side_effects=True, vmem_limit_bytes=48 * 2**20
        ),
        name="fused_backward",
    )(
        place,
        place_t,
        local,
        token_input_rows,
        output_gradient_rows,
        key_matrix,
        adapter_down_weight,
        adapter_up_weight,
    )


def shards(
    token_input_rows,
    output_gradient_rows,
    token_tenant_index,
    tenant_slot_index,
    key_matrix,
    adapter_down_weight,
    adapter_up_weight,
):
    holders = lax.axis_size("owner")
    row_count = token_input_rows.shape[0]
    feat_width = token_input_rows.shape[1]
    grad_width = output_gradient_rows.shape[1]
    capacity = 2 * row_count // holders
    total_slots = holders * capacity
    slot_of = tenant_slot_index[token_tenant_index]
    target = slot_of // TEN_DEV
    local_index = slot_of % TEN_DEV
    onehot = (target[:, None] == jnp.arange(holders, dtype=jnp.int32)[None, :]).astype(jnp.int32)
    earlier = jnp.cumsum(onehot, axis=0) - onehot
    bucket_place = target * capacity + jnp.sum(earlier * onehot, axis=1)
    send_x = (
        jnp.zeros((total_slots, feat_width), jnp.bfloat16)
        .at[bucket_place]
        .set(token_input_rows)
        .reshape(holders, capacity, feat_width)
    )
    send_g = (
        jnp.zeros((total_slots, grad_width), jnp.bfloat16)
        .at[bucket_place]
        .set(output_gradient_rows)
        .reshape(holders, capacity, grad_width)
    )
    send_id = (
        jnp.full((total_slots,), -1, jnp.int32)
        .at[bucket_place]
        .set(local_index)
        .reshape(holders, capacity)
    )
    received_input, received_gradient, received_tenant = (
        lax.all_to_all(send_x, "owner", split_axis=0, concat_axis=0, tiled=True),
        lax.all_to_all(send_g, "owner", split_axis=0, concat_axis=0, tiled=True),
        lax.all_to_all(send_id, "owner", split_axis=0, concat_axis=0, tiled=True),
    )
    adapter_part, down_grads, up_grads = slot_holder_products(
        received_input.reshape(total_slots, feat_width),
        received_gradient.reshape(total_slots, grad_width),
        received_tenant.reshape(total_slots),
        adapter_down_weight,
        adapter_up_weight,
    )
    returned = lax.all_to_all(
        adapter_part.reshape(holders, capacity, feat_width),
        "owner",
        split_axis=0,
        concat_axis=0,
        tiled=True,
    )
    mine = returned.reshape(total_slots, feat_width)[bucket_place]
    base = frozen_product(output_gradient_rows, key_matrix)
    input_grads = (base + mine.astype(jnp.float32)).astype(jnp.bfloat16)
    return (input_grads, down_grads, up_grads)


def solution(mesh):
    on_grid = mesh.shape["groups"] == 2 and mesh.shape["owner"] == 4 * LAYERS
    return jax.shard_map(
        fused_shards if on_grid else shards,
        mesh=mesh,
        in_specs=(
            P(("groups", "owner"), None),
            P(("groups", "owner"), None),
            P(("groups", "owner")),
            P("groups"),
            P("owner", None),
            P(None, ("groups", "owner")),
            P(("groups", "owner"), None),
        ),
        out_specs=(
            P(("groups", "owner"), None),
            P(None, ("groups", "owner")),
            P(("groups", "owner"), None),
        ),
        check_vma=False,
    )
```
